32 devices in a mesh: dp: 8 (over z, x), mp: 4 (over y, core).
Axes of the slice: x: 2, y: 2, z: 4, core: 2. Of those that a mesh axis runs over, the one named last changes fastest.
Arguments:
- hidden_in: bfloat16 [1024, 16384], P('mp', 'dp'), may hold values from -6 to 6
- segment_ids: int32 [16384], P('dp'), may hold values from 0 to 15, never falling along the last dimension, each value on 1 to 2000 neighbouring positions
- w_query: bfloat16 [1024, 1024], P(None, 'mp'), may hold values from -0.1875 to 0.1875
- b_query: bfloat16 [1024], P('mp'), may hold values from -3 to 3
- w_key: bfloat16 [1024, 1024], P(None, 'mp'), may hold values from -0.1875 to 0.1875
- w_value: bfloat16 [1024, 1024], P(None, 'mp'), may hold values from -0.1875 to 0.1875
- b_value: bfloat16 [1024], P('mp'), may hold values from -3 to 3
- w_out: bfloat16 [1024, 1024], P('mp'), may hold values from -3 to 3
- b_out: bfloat16 [1024], P('mp'), may hold values from -3 to 3
- gain_one: bfloat16 [1024], P('mp'), may hold values from 0.25 to 1.75
- shift_one: bfloat16 [1024], P('mp'), may hold values from -3 to 3
- w_up: bfloat16 [1024, 4096], P(None, 'mp'), may hold values from -0.1875 to 0.1875
- b_up: bfloat16 [4096], P('mp'), may hold values from -3 to 3
- w_down: bfloat16 [4096, 1024], P('mp'), may hold values from -0.09375 to 0.09375
- b_down: bfloat16 [1024], P('mp'), may hold values from -3 to 3
- gain_two: bfloat16 [1024], P('mp'), may hold values from 0.25 to 1.75
- shift_two: bfloat16 [1024], P('mp'), may hold values from -3 to 3
- cotangent: bfloat16 [1024, 16384], P('mp', 'dp'), may hold values from -6 to 6
Outputs:
- layer_out: bfloat16 [1024, 16384], P('mp', 'dp')
- input_grad: bfloat16 [1024, 16384], P('mp', 'dp')
- grad_w_query: float32 [1024, 1024], P(None, 'mp')
- grad_b_query: float32 [1024], P('mp')
- grad_w_key: float32 [1024, 1024], P(None, 'mp')
- grad_w_value: float32 [1024, 1024], P(None, 'mp')
- grad_b_value: float32 [1024], P('mp')
- grad_w_out: float32 [1024, 1024], P('mp')
- grad_b_out: float32 [1024], P('mp')
- grad_gain_one: float32 [1024], P('mp')
- grad_shift_one: float32 [1024], P('mp')
- grad_w_up: float32 [1024, 4096], P(None, 'mp')
- grad_b_up: float32 [4096], P('mp')
- grad_w_down: float32 [4096, 1024], P('mp')
- grad_b_down: float32 [1024], P('mp')
- grad_gain_two: float32 [1024], P('mp')
- grad_shift_two: float32 [1024], P('mp')
The draws below stay inside these ranges and needn't reach their ends.
Inputs may be any that keep to these rules, and one draw needn't show every extreme that they name: `segment_ids`: document numbers never fall along the tokens; each of the 16 numbers occurs on 1 to 2000 consecutive tokens, and some document has exactly 2000. A document may cross the border of two sequences; attention never does.
All inputs are finite; a program needn't handle non-finite values.
Results may differ from the reference program's by a relative error of at most 0.02.
Values may be sent and summed in bfloat16 or wider, within the bound.
No kernel may reach another device: no remote copies, remote signals or barrier semaphores. Data moves between devices by JAX's collectives and lax.ppermute only.
A program may use at most 384 MiB of HBM per device.

```python
import math
import jax
import jax.numpy as jnp
import numpy as np
from jax import lax

D = 1024
HEADS = 16
HEAD = 64
FF = 4096
SEQ_LEN = 2048
DOC_MOST = 2000
TOKENS = 16384
DOC_COUNT = 16


def level_of(key, dims, cuts, least, top_value):
    def one(dim, parts):
        heights = jax.random.uniform(jax.random.fold_in(jax.random.fold_in(key, 6), dim), (parts,), jnp.float32, least / len(cuts), top_value / len(cuts))
        return jnp.repeat(jnp.exp(heights), dims[dim] // parts).reshape((-1,) + (1,) * (len(dims) - dim - 1))

    gain = one(*cuts[0])
    for cut in cuts[1:]:
        gain = gain * one(*cut)
    return gain


def split_up(amount, total, bound, skew):
    loads = [(1 << 20) // math.isqrt(standing ** skew) + 1 for standing in range(2, amount + 1)]
    rest, counts = total - bound - (amount - 1), [1] * (amount - 1)
    while rest > 0:
        movable = [i for i in range(amount - 1) if counts[i] < bound]
        whole, left = sum([loads[i] for i in movable]), rest
        for i in movable:
            addition = min(bound - counts[i], max(1, left * loads[i] // whole), rest)
            counts[i] = counts[i] + addition
            rest = rest - addition
    return np.array([bound] + counts)


def uneven_parts(stream_key, amount, total, most, slope):
    if amount == 2:
        one = jax.random.randint(stream_key, (), max(1, total - most), min(most, total - 1) + 1)
        return jnp.stack([one, total - one])
    sizes = jnp.asarray(split_up(amount, total, most, slope), jnp.int32)
    pairs = (amount - 1) // 2
    giver, taker = sizes[1:1 + 2 * pairs:2], sizes[2:2 + 2 * pairs:2]
    margin = jnp.minimum(giver - 1, most - taker)
    moved = jax.random.randint(jax.random.fold_in(stream_key, 1), (pairs,), 0, 1 << 20) % (margin + 1)
    sizes = sizes.at[1:1 + 2 * pairs:2].set(giver - moved).at[2:2 + 2 * pairs:2].set(taker + moved)
    return sizes[jax.random.permutation(jax.random.fold_in(stream_key, 2), amount)]


def centred(rng, dims, deviation, bound, shards=(), kind=jnp.bfloat16):
    values = jax.random.normal(rng, dims, jnp.float32) * deviation
    if len(shards) > 0:
        values = level_of(rng, dims, shards, -0.22, 0.18) * values
    return jnp.clip(values, min=-bound, max=bound).astype(kind)


def setup_inputs(seed: int = 0) -> dict:
    seeds = jax.random.split(jax.random.key(seed), 19)
    return {
        "hidden_in": centred(seeds[0], (D, TOKENS), 1.0, 6.0, ((0, 4), (1, 8))),
        "segment_ids": jnp.searchsorted(jnp.cumsum(uneven_parts(seeds[1], DOC_COUNT, TOKENS, DOC_MOST, 2)), jnp.arange(TOKENS), side="right").astype(jnp.int32),
        "w_query": centred(seeds[2], (D, D), D ** -0.5, 0.1875, ((1, 4),)),
        "b_query": centred(seeds[3], (D,), 0.5, 3.0, ((0, 4),)),
        "w_key": centred(seeds[4], (D, D), D ** -0.5, 0.1875, ((1, 4),)),
        "w_value": centred(seeds[5], (D, D), D ** -0.5, 0.1875, ((1, 4),)),
        "b_value": centred(seeds[6], (D,), 0.5, 3.0, ((0, 4),)),
        "w_out": centred(seeds[7], (D, D), (max(D // 256, 2)) ** -0.5, 3.0, ((0, 4),)),
        "b_out": centred(seeds[8], (D,), 0.5, 3.0, ((0, 4),)),
        "gain_one": jnp.clip(1.0 + 0.15 * jax.random.normal(seeds[9], (D,), jnp.float32), 0.25, 1.75).astype(jnp.bfloat16),
        "shift_one": centred(seeds[10], (D,), 0.5, 3.0, ((0, 4),)),
        "w_up": centred(seeds[11], (D, FF), D ** -0.5, 0.1875, ((1, 4),)),
        "b_up": centred(seeds[12], (FF,), 0.5, 3.0, ((0, 4),)),
        "w_down": centred(seeds[13], (FF, D), FF ** -0.5, 0.09375, ((0, 4),)),
        "b_down": centred(seeds[14], (D,), 0.5, 3.0, ((0, 4),)),
        "gain_two": jnp.clip(1.0 + 0.15 * jax.random.normal(seeds[15], (D,), jnp.float32), 0.25, 1.75).astype(jnp.bfloat16),
        "shift_two": centred(seeds[16], (D,), 0.5, 3.0, ((0, 4),)),
        "cotangent": centred(seeds[17], (D, TOKENS), 1.0, 6.0, ((0, 4), (1, 8))),
    }


EPS = 1e-05
NEG = -1e+30

@jax.custom_vjp
def low(v):
    return lax.optimization_barrier(v.astype(jnp.bfloat16)).astype(jnp.float32)

@jax.custom_vjp
def low_back(v):
    return v

def low_keep(v):
    return (low(v), None)

def low_pass(kept, grad):
    return (grad,)

def back_keep(v):
    return (v, None)

def back_low(kept, grad):
    return (low(grad),)
low.defvjp(low_keep, low_pass)
low_back.defvjp(back_keep, back_low)

def product(left, right):
    return jnp.dot(left, right, precision=lax.Precision.HIGHEST)

def layer_norm(values, norm_gain, norm_shift):
    centre = values - lax.optimization_barrier(jnp.mean(values, axis=-1, keepdims=True))
    spread = lax.optimization_barrier(jnp.mean(centre * centre, axis=-1, keepdims=True))
    return centre * lax.rsqrt(spread + EPS) * norm_gain + norm_shift

def layer(params, inputs, segments):
    w_query, b_query, w_key, w_value, b_value, w_out, b_out, gain_one, shift_one, w_up, b_up, w_down, b_down, gain_two, shift_two = params
    length = inputs.shape[0]
    queries = low(low_back(product(inputs, w_query) + b_query))
    keys_all = low(low_back(product(inputs, w_key)))
    values_all = low(low_back(product(inputs, w_value) + b_value))
    allowed = segments[:, None] == segments[None, :]
    factor = 1.0 / math.sqrt(HEAD)

    def split_heads(stacked):
        return stacked.reshape(length, HEADS, HEAD).transpose(1, 0, 2)

    def one_head(triple):
        head_q, head_k, head_v = triple
        scores = low_back(jnp.where(allowed, product(head_q, head_k.T) * factor, NEG))
        softened = jax.nn.softmax(scores, axis=-1)
        return product(low(softened), head_v)
    context = lax.map(jax.checkpoint(one_head), (split_heads(queries), split_heads(keys_all), split_heads(values_all)))
    context = low(low_back(context.transpose(1, 0, 2).reshape(length, D)))
    normed_first = layer_norm(inputs + (low_back(product(context, w_out)) + b_out), gain_one, shift_one)
    upward = low_back(product(low(normed_first), w_up) + b_up)
    activated = low(jax.nn.gelu(upward, approximate=False))
    return layer_norm(normed_first + (low_back(product(activated, w_down)) + b_down), gain_two, shift_two)

def reference(hidden_in, segment_ids, w_query, b_query, w_key, w_value, b_value, w_out, b_out, gain_one, shift_one, w_up, b_up, w_down, b_down, gain_two, shift_two, cotangent):
    params = tuple((weight_arg.astype(jnp.float32) for weight_arg in (w_query, b_query, w_key, w_value, b_value, w_out, b_out, gain_one, shift_one, w_up, b_up, w_down, b_down, gain_two, shift_two)))
    seq_count = TOKENS // SEQ_LEN
    inputs_all = hidden_in.astype(jnp.float32).T.reshape(seq_count, SEQ_LEN, D)
    cot_all = cotangent.astype(jnp.float32).T.reshape(seq_count, SEQ_LEN, D)
    seg_all = segment_ids.reshape(seq_count, SEQ_LEN)

    def per_sequence(totals, pieces):
        inputs, cot_rows, segments = pieces
        result, pullback = jax.vjp(lambda weights, rows_in: layer(weights, rows_in, segments), params, inputs)
        weight_grads, input_grads = pullback(cot_rows)
        return (jax.tree.map(jnp.add, totals, weight_grads), (result, input_grads))
    zero_grads = jax.tree.map(jnp.zeros_like, params)
    totals, (outputs, input_grads) = lax.scan(per_sequence, zero_grads, (inputs_all, cot_all, seg_all))
    layer_out = outputs.reshape(TOKENS, D).T.astype(jnp.bfloat16)
    input_grad = input_grads.reshape(TOKENS, D).T.astype(jnp.bfloat16)
    grad_w_query, grad_b_query, grad_w_key, grad_w_value, grad_b_value, grad_w_out, grad_b_out, grad_gain_one, grad_shift_one, grad_w_up, grad_b_up, grad_w_down, grad_b_down, grad_gain_two, grad_shift_two = totals
    return (layer_out, input_grad, grad_w_query, grad_b_query, grad_w_key, grad_w_value, grad_b_value, grad_w_out, grad_b_out, grad_gain_one, grad_shift_one, grad_w_up, grad_b_up, grad_w_down, grad_b_down, grad_gain_two, grad_shift_two)
```

```python
import math

import jax
import jax.numpy as jnp
from jax import lax
from jax.experimental import pallas as pl
from jax.experimental.pallas import tpu as pltpu
from jax.sharding import PartitionSpec as P

D = 1024
HEADS = 16
HEAD = 64
SEQ_LEN = 2048

EPS = 1e-05
BIG = 1e30
Q_BLOCK = 256
K_CHUNK = 512
VMEM_LIMIT = 56 * 1024 * 1024

F32 = jnp.float32
BF16 = jnp.bfloat16


def lead_dot(left, right):
    return lax.dot_general(left, right, (((0,), (0,)), ((), ())), preferred_element_type=F32)


def tail_dot(left, right):
    return lax.dot_general(left, right, (((1,), (1,)), ((), ())), preferred_element_type=F32)


def dot(left, right):
    return jnp.dot(left, right, preferred_element_type=F32)


def swap(piece, axis, mask):
    count = lax.axis_size(axis)
    return lax.ppermute(piece, axis, [(i, i ^ mask) for i in range(count)])


def bits_of(axis):
    count, found, bit = lax.axis_size(axis), [], 1
    while bit < count:
        found.append(bit)
        bit *= 2
    return found


def gather_slots(piece, axis):
    slots = {0: piece}
    for bit in reversed(bits_of(axis)):
        for slot in sorted(slots):
            slots[slot | bit] = swap(slots[slot], axis, bit)
    return slots


def scatter_slots(slots, axis, wire=BF16):
    slots = dict(slots)
    for bit in bits_of(axis):
        for slot in sorted(slots, reverse=True):
            if slot & bit:
                moved = swap(slots.pop(slot).astype(wire), axis, bit)
                slots[slot ^ bit] = slots[slot ^ bit].astype(F32) + moved.astype(F32)
    return slots[0]


def place(slots, own, dim):
    count, width = len(slots), slots[0].shape[dim]
    shape = list(slots[0].shape)
    shape[dim] = width * count
    whole = jnp.zeros(shape, slots[0].dtype)
    for slot in sorted(slots):
        whole = lax.dynamic_update_slice_in_dim(whole, slots[slot], (own ^ slot) * width, dim)
    return whole


def cut(whole, own, slot, count, dim):
    width = whole.shape[dim] // count
    return lax.dynamic_slice_in_dim(whole, (own ^ slot) * width, width, dim)


def exchange(whole, own, axis, dim):
    count = lax.axis_size(axis)
    return {
        slot: swap(cut(whole, own, slot, count, dim), axis, slot)
        if slot
        else cut(whole, own, 0, count, dim)
        for slot in range(count)
    }


def sum_over(piece, axis, order):
    index = lax.axis_index(axis)
    trail = []
    for bit in order:
        upper = (index & bit) != 0
        half = piece.shape[0] // 2
        mine = lax.dynamic_slice_in_dim(piece, jnp.where(upper, half, 0), half, 0)
        other = lax.dynamic_slice_in_dim(piece, jnp.where(upper, 0, half), half, 0)
        got = swap(other, axis, bit)
        piece = (mine.astype(F32) + got.astype(F32)).astype(piece.dtype)
        trail.append((bit, upper))
    for bit, upper in reversed(trail):
        got = swap(piece, axis, bit)
        half = piece.shape[0]
        whole = jnp.concatenate([piece, piece], axis=0)
        piece = lax.dynamic_update_slice_in_dim(whole, got, jnp.where(upper, 0, half), 0)
    return piece


def sum_small(piece, axis):
    for bit in bits_of(axis):
        piece = piece + swap(piece, axis, bit)
    return piece


def sum_weights(piece, axis):
    order = bits_of(axis)
    rows = piece.shape[0] // 2
    return jnp.concatenate(
        [
            sum_over(piece[:rows], axis, order),
            sum_over(piece[rows:], axis, order[1:] + order[:1]),
        ],
        axis=0,
    )


def seg_codes(segment_ids):
    digits = jnp.arange(16, dtype=jnp.int32)[:, None]
    low = (segment_ids[None, :] & 15) == digits
    high = ((segment_ids[None, :] >> 4) & 15) == digits
    same = jnp.concatenate([low, high], axis=0)
    keys = same.astype(BF16)
    queries = jnp.where(same, 0.0, -BIG).astype(BF16)
    return keys, queries


def key_ranges(segment_ids, seq_count):
    rows = segment_ids.reshape(seq_count, 1, SEQ_LEN)
    blocks = segment_ids.reshape(seq_count, SEQ_LEN // Q_BLOCK, Q_BLOCK)
    first = jnp.sum((rows < blocks[:, :, :1]).astype(jnp.int32), axis=-1)
    last = jnp.sum((rows <= blocks[:, :, -1:]).astype(jnp.int32), axis=-1)
    return (first // K_CHUNK).reshape(-1), ((last + K_CHUNK - 1) // K_CHUNK).reshape(-1)


def attend_kernel(heads, from_ref, to_ref, q_ref, k_ref, v_ref, qc_ref, kc_ref, o_ref, lse_ref, kt, va, top, acc):
    seq, block = pl.program_id(0), pl.program_id(1)
    spot = seq * pl.num_programs(1) + block

    @pl.when(block == 0)
    def _():
        codes = kc_ref[...].astype(F32)
        for h in range(heads):
            rows = slice(h * HEAD, (h + 1) * HEAD)
            whole = jnp.concatenate([k_ref[rows, :].astype(F32), codes, jnp.zeros_like(codes)], axis=0)
            kt[h] = whole.T.astype(BF16)
            lines = lax.broadcasted_iota(jnp.int32, (16, SEQ_LEN), 0)
            va[h] = jnp.concatenate(
                [v_ref[rows, :], jnp.where(lines == 0, 1.0, 0.0).astype(BF16)], axis=0
            )

    top[...] = jnp.full_like(top, -BIG)
    acc[...] = jnp.zeros_like(acc)
    queries = []
    for h in range(heads):
        scaled = (q_ref[h * HEAD : (h + 1) * HEAD, :].astype(F32) * (1.0 / math.sqrt(HEAD))).astype(BF16)
        queries.append(
            jnp.concatenate([scaled, qc_ref[...], jnp.zeros((32, Q_BLOCK), BF16)], axis=0)
        )

    def step(chunk, carry):
        at = pl.multiple_of(chunk * K_CHUNK, K_CHUNK)
        for h in range(heads):
            scores = dot(kt[h, pl.ds(at, K_CHUNK), :], queries[h])
            before = top[h]
            highest = jnp.maximum(before, jnp.max(scores, axis=0, keepdims=True))
            raised = jnp.exp(scores - highest).astype(BF16)
            acc[h] = acc[h] * jnp.exp(before - highest) + dot(va[h, :, pl.ds(at, K_CHUNK)], raised)
            top[h] = highest
        return carry

    lax.fori_loop(from_ref[spot], to_ref[spot], step, 0)
    for h in range(heads):
        total = acc[h, HEAD : HEAD + 1, :]
        o_ref[h * HEAD : (h + 1) * HEAD, :] = (acc[h, :HEAD, :] / total).astype(BF16)
        lse_ref[0, h : h + 1, :] = top[h] + jnp.log(total)


def attend(queries, keys, values, codes_q, codes_k, ranges, seq_count):
    width, length = queries.shape
    heads = width // HEAD
    blocks = SEQ_LEN // Q_BLOCK
    by_block = lambda s, b, *_: (0, s * blocks + b)
    by_seq = lambda s, b, *_: (0, s)
    spec = pltpu.PrefetchScalarGridSpec(
        num_scalar_prefetch=2,
        grid=(seq_count, blocks),
        in_specs=[
            pl.BlockSpec((width, Q_BLOCK), by_block),
            pl.BlockSpec((width, SEQ_LEN), by_seq),
            pl.BlockSpec((width, SEQ_LEN), by_seq),
            pl.BlockSpec((32, Q_BLOCK), by_block),
            pl.BlockSpec((32, SEQ_LEN), by_seq),
        ],
        out_specs=[
            pl.BlockSpec((width, Q_BLOCK), by_block),
            pl.BlockSpec((1, heads, Q_BLOCK), lambda s, b, *_: (0, 0, s * blocks + b)),
        ],
        scratch_shapes=[
            pltpu.VMEM((heads, SEQ_LEN, 128), BF16),
            pltpu.VMEM((heads, HEAD + 16, SEQ_LEN), BF16),
            pltpu.VMEM((heads, 1, Q_BLOCK), F32),
            pltpu.VMEM((heads, HEAD + 16, Q_BLOCK), F32),
        ],
    )
    area = length * SEQ_LEN * heads
    return pl.pallas_call(
        lambda *refs: attend_kernel(heads, *refs),
        grid_spec=spec,
        out_shape=[
            jax.ShapeDtypeStruct((width, length), BF16),
            jax.ShapeDtypeStruct((1, heads, length), F32),
        ],
        compiler_params=pltpu.CompilerParams(
            dimension_semantics=("arbitrary", "arbitrary"), vmem_limit_bytes=VMEM_LIMIT
        ),
        cost_estimate=pl.CostEstimate(flops=12 * HEAD * area, bytes_accessed=8 * width * length, transcendentals=area),
        name="attend",
    )(*ranges, queries, keys, values, codes_q, codes_k)


def attend_back_kernel(
    heads, from_ref, to_ref, q_ref, o_ref, do_ref, lse_ref, k_ref, v_ref, qc_ref, kc_ref, dq_ref, dkv_ref, kt, vt, acc, dq_acc
):
    seq, block = pl.program_id(0), pl.program_id(1)
    spot = seq * pl.num_programs(1) + block

    @pl.when(block == 0)
    def _():
        codes = kc_ref[...].astype(F32)
        lines = lax.broadcasted_iota(jnp.int32, (16, SEQ_LEN), 0)
        ones = jnp.where(lines < 3, 1.0, 0.0).astype(F32)
        blank = jnp.zeros((16, SEQ_LEN), F32)
        for h in range(heads):
            rows = slice(h * HEAD, (h + 1) * HEAD)
            kt[h] = jnp.concatenate([k_ref[rows, :].astype(F32), codes, ones, blank], axis=0).T.astype(BF16)
            vt[h] = jnp.concatenate([v_ref[rows, :].astype(F32), ones, blank, blank, blank], axis=0).T.astype(BF16)
        acc[...] = jnp.zeros_like(acc)

    dq_acc[...] = jnp.zeros_like(dq_acc)
    lines = lax.broadcasted_iota(jnp.int32, (16, Q_BLOCK), 0)
    lanes = lax.broadcasted_iota(jnp.int32, (Q_BLOCK, 128), 1)
    blank = jnp.zeros((16, Q_BLOCK), BF16)

    def parts(row):
        first = row.astype(BF16)
        rest = row - first.astype(F32)
        second = rest.astype(BF16)
        third = (rest - second.astype(F32)).astype(BF16)
        spread = jnp.where(
            lines == 0,
            first.astype(F32),
            jnp.where(lines == 1, second.astype(F32), jnp.where(lines == 2, third.astype(F32), 0.0)),
        )
        return spread.astype(BF16)

    queries, grads, both = [], [], []
    for h in range(heads):
        rows = slice(h * HEAD, (h + 1) * HEAD)
        scaled = q_ref[rows, :].astype(F32) * (1.0 / math.sqrt(HEAD))
        grad = do_ref[rows, :].astype(F32)
        centre = jnp.sum(grad * o_ref[rows, :].astype(F32), axis=0, keepdims=True)
        queries.append(
            jnp.concatenate([scaled.astype(BF16), qc_ref[...], parts(-lse_ref[0, h : h + 1, :]), blank], axis=0)
        )
        grads.append(jnp.concatenate([do_ref[rows, :], parts(-centre), blank, blank, blank], axis=0))
        turned = jnp.concatenate([grad, scaled], axis=0).T
        both.append(
            jnp.concatenate(
                [jnp.where(lanes < HEAD, turned, 0.0), jnp.where(lanes < HEAD, 0.0, turned)], axis=0
            ).astype(BF16)
        )

    def step(chunk, carry):
        at = pl.multiple_of(chunk * K_CHUNK, K_CHUNK)
        span = pl.ds(at, K_CHUNK)
        for h in range(heads):
            softened = jnp.exp(dot(kt[h, span, :], queries[h]))
            shifted = dot(vt[h, span, :], grads[h])
            score_grad = (softened * shifted).astype(BF16)
            pair = jnp.concatenate([softened.astype(BF16), score_grad], axis=1)
            acc[h, span, :] += dot(pair, both[h])
            dq_acc[h] += dot(k_ref[h * HEAD : (h + 1) * HEAD, span], score_grad)
        return carry

    lax.fori_loop(from_ref[spot], to_ref[spot], step, 0)
    for h in range(heads):
        dq_ref[h * HEAD : (h + 1) * HEAD, :] = (dq_acc[h] * (1.0 / math.sqrt(HEAD))).astype(BF16)

    @pl.when(block == pl.num_programs(1) - 1)
    def _():
        for h in range(heads):
            dkv_ref[:, h * 128 : (h + 1) * 128] = acc[h].astype(BF16)


def attend_back(queries, context, grads, log_totals, keys, values, codes_q, codes_k, ranges, seq_count):
    width, length = queries.shape
    heads = width // HEAD
    blocks = SEQ_LEN // Q_BLOCK
    by_block = lambda s, b, *_: (0, s * blocks + b)
    by_seq = lambda s, b, *_: (0, s)
    spec = pltpu.PrefetchScalarGridSpec(
        num_scalar_prefetch=2,
        grid=(seq_count, blocks),
        in_specs=[
            pl.BlockSpec((width, Q_BLOCK), by_block),
            pl.BlockSpec((width, Q_BLOCK), by_block),
            pl.BlockSpec((width, Q_BLOCK), by_block),
            pl.BlockSpec((1, heads, Q_BLOCK), lambda s, b, *_: (0, 0, s * blocks + b)),
            pl.BlockSpec((width, SEQ_LEN), by_seq),
            pl.BlockSpec((width, SEQ_LEN), by_seq),
            pl.BlockSpec((32, Q_BLOCK), by_block),
            pl.BlockSpec((32, SEQ_LEN), by_seq),
        ],
        out_specs=[
            pl.BlockSpec((width, Q_BLOCK), by_block),
            pl.BlockSpec((SEQ_LEN, 2 * width), lambda s, b, *_: (s, 0)),
        ],
        scratch_shapes=[
            pltpu.VMEM((heads, SEQ_LEN, 128), BF16),
            pltpu.VMEM((heads, SEQ_LEN, 128), BF16),
            pltpu.VMEM((heads, SEQ_LEN, 128), F32),
            pltpu.VMEM((heads, HEAD, Q_BLOCK), F32),
        ],
    )
    area = length * SEQ_LEN * heads
    return pl.pallas_call(
        lambda *refs: attend_back_kernel(heads, *refs),
        grid_spec=spec,
        out_shape=[
            jax.ShapeDtypeStruct((width, length), BF16),
            jax.ShapeDtypeStruct((length, 2 * width), BF16),
        ],
        compiler_params=pltpu.CompilerParams(
            dimension_semantics=("arbitrary", "arbitrary"), vmem_limit_bytes=VMEM_LIMIT
        ),
        cost_estimate=pl.CostEstimate(flops=30 * HEAD * area, bytes_accessed=14 * width * length, transcendentals=area),
        name="attend_back",
    )(*ranges, queries, context, grads, log_totals, keys, values, codes_q, codes_k)


def norm_rows(values, norm_gain, norm_shift):
    centre = values - jnp.mean(values, axis=0, keepdims=True)
    inverse = lax.rsqrt(jnp.mean(centre * centre, axis=0, keepdims=True) + EPS)
    normed = centre * inverse
    return (normed * norm_gain[:, None] + norm_shift[:, None], normed, inverse)


def norm_back(grad_rows, normed, inverse, norm_gain):
    scaled = grad_rows * norm_gain[:, None]
    return inverse * (
        scaled
        - jnp.mean(scaled, axis=0, keepdims=True)
        - normed * jnp.mean(scaled * normed, axis=0, keepdims=True)
    )


def gelu_slope(upward):
    flat = (1.0 + lax.erf(upward * (1.0 / math.sqrt(2.0)))) * 0.5
    return flat + upward * jnp.exp(upward * upward * -0.5) * (1.0 / math.sqrt(2.0 * math.pi))


def body(
    hidden_in,
    segment_ids,
    w_query,
    b_query,
    w_key,
    w_value,
    b_value,
    w_out,
    b_out,
    gain_one,
    shift_one,
    w_up,
    b_up,
    w_down,
    b_down,
    gain_two,
    shift_two,
    cotangent,
):
    parts = lax.axis_size("mp")
    own = lax.axis_index("mp")
    width, length = hidden_in.shape
    seq_count = length // SEQ_LEN
    own_len = length // parts
    own_heads = width // HEAD

    inputs = place(gather_slots(hidden_in, "mp"), own, 0)
    vectors = jnp.stack([b_out, gain_one, shift_one, b_down, gain_two, shift_two])
    vectors = place(gather_slots(vectors, "mp"), own, 1).astype(F32)
    bias_out, gain_first, shift_first, bias_down, gain_second, shift_second = [vectors[i] for i in range(6)]
    out_slots = gather_slots(w_out, "mp")
    full_out = jnp.concatenate([out_slots[r] for r in range(parts)], axis=0)
    cot_own = place(exchange(cotangent, own, "mp", 1), own, 0)

    w_pair = jnp.concatenate(
        [w_value.reshape(D, own_heads, HEAD), w_key.reshape(D, own_heads, HEAD)], axis=2
    ).reshape(D, 2 * width)
    queries = (lead_dot(w_query, inputs) + b_query.astype(F32)[:, None]).astype(BF16)
    keys = lead_dot(w_key, inputs).astype(BF16)
    values = (lead_dot(w_value, inputs) + b_value.astype(F32)[:, None]).astype(BF16)
    codes_k, codes_q = seg_codes(segment_ids)
    ranges = key_ranges(segment_ids, seq_count)
    context, log_totals = attend(queries, keys, values, codes_q, codes_k, ranges, seq_count)

    context_slots = exchange(context, own, "mp", 1)
    context_own = jnp.concatenate([context_slots[r] for r in range(parts)], axis=0)
    inputs_own = lax.dynamic_slice_in_dim(inputs, own * own_len, own_len, 1)
    first_sum = inputs_own.astype(F32) + (lead_dot(full_out, context_own) + bias_out[:, None])
    first_out, normed_first, inverse_one = norm_rows(first_sum, gain_first, shift_first)

    first_low = gather_slots(first_out.astype(BF16), "mp")
    bias_up = b_up.astype(F32)[:, None]
    upward, activated, down_part = {}, {}, {}
    for r in range(parts):
        upward[r] = lead_dot(w_up, first_low[r]) + bias_up
        activated[r] = jax.nn.gelu(upward[r], approximate=False).astype(BF16)
        down_part[r] = lead_dot(w_down, activated[r])
        if r:
            down_part[r] = down_part[r].astype(BF16)
    second_sum = first_out + (scatter_slots(down_part, "mp") + bias_down[:, None])
    final_rows, normed_second, inverse_two = norm_rows(second_sum, gain_second, shift_second)
    layer_out = place(exchange(final_rows.astype(BF16), own, "mp", 0), own, 1)

    grad_rows = cot_own.astype(F32)
    grad_shift_two = jnp.sum(grad_rows, axis=1)
    grad_gain_two = jnp.sum(grad_rows * normed_second, axis=1)
    second_grad = norm_back(grad_rows, normed_second, inverse_two, gain_second)
    grad_b_down = jnp.sum(second_grad, axis=1)

    down_low = gather_slots(second_grad.astype(BF16), "mp")
    up_low, up_part = {}, {}
    for r in range(parts):
        up_low[r] = (dot(w_down, down_low[r]) * gelu_slope(upward[r])).astype(BF16)
        up_part[r] = dot(w_up, up_low[r])
        if r:
            up_part[r] = up_part[r].astype(BF16)
    joined = lambda slots: jnp.concatenate([slots[r] for r in range(parts)], axis=1)
    all_up = joined(up_low)
    grad_w_down = tail_dot(joined(activated), joined(down_low)).astype(BF16)
    grad_w_up = tail_dot(joined(first_low), all_up).astype(BF16)
    grad_b_up = jnp.sum(all_up.astype(F32), axis=1)
    sum_down = sum_weights(grad_w_down, "dp")
    sum_up = sum_weights(grad_w_up, "dp")

    first_grad = second_grad + scatter_slots(up_part, "mp")
    grad_shift_one = jnp.sum(first_grad, axis=1)
    grad_gain_one = jnp.sum(first_grad * normed_first, axis=1)
    attn_grad = norm_back(first_grad, normed_first, inverse_one, gain_first)
    grad_b_out = jnp.sum(attn_grad, axis=1)
    out_low = attn_grad.astype(BF16)
    context_grad = dot(full_out, out_low).astype(BF16)
    grad_heads = place(
        {r: swap(context_grad[r * width : (r + 1) * width], "mp", r) if r else context_grad[:width] for r in range(parts)},
        own,
        1,
    )
    out_part = tail_dot(context_own, out_low).astype(BF16)
    grad_w_out = scatter_slots({r: out_part[r * width : (r + 1) * width] for r in range(parts)}, "mp")
    sum_out = sum_weights(grad_w_out.astype(BF16), "dp")

    query_grad, pair_grad = attend_back(
        queries, context, grad_heads, log_totals, keys, values, codes_q, codes_k, ranges, seq_count
    )
    grad_b_query = jnp.sum(query_grad.astype(F32), axis=1)
    grad_pair = dot(inputs, pair_grad)
    grad_pair_bias = jnp.sum(pair_grad.astype(F32), axis=0)
    grad_w_query = tail_dot(inputs, query_grad)
    split_pair = grad_pair.reshape(D, own_heads, 2, HEAD)
    grad_w_value = split_pair[:, :, 0].reshape(D, width)
    grad_w_key = split_pair[:, :, 1].reshape(D, width)
    grad_b_value = grad_pair_bias.reshape(own_heads, 2, HEAD)[:, 0].reshape(width)

    input_part = {}
    for r in range(parts):
        rows_query = cut(w_query, own, r, parts, 0)
        rows_pair = cut(w_pair, own, r, parts, 0)
        part = dot(rows_query, query_grad) + tail_dot(rows_pair, pair_grad)
        low = part.astype(BF16)
        here = lax.dynamic_slice_in_dim(low, own * own_len, own_len, 1).astype(F32) + cut(attn_grad, own, r, parts, 0)
        input_part[r] = lax.dynamic_update_slice_in_dim(low, here.astype(BF16), own * own_len, 1)
    input_grad = scatter_slots(input_part, "mp").astype(BF16)

    sum_heads = sum_weights(jnp.concatenate([grad_w_query, grad_w_key, grad_w_value], axis=0).astype(BF16), "dp")

    mixed = jnp.stack([grad_b_out, grad_gain_one, grad_shift_one, grad_b_down, grad_gain_two, grad_shift_two])
    mixed = scatter_slots({r: cut(mixed, own, r, parts, 1) for r in range(parts)}, "mp", wire=F32)
    small = jnp.concatenate([mixed.reshape(-1), grad_b_query, grad_b_value, grad_b_up])
    small = sum_small(small, "dp")
    vec = [small[i * width : (i + 1) * width] for i in range(8)]
    return (
        layer_out,
        input_grad,
        sum_heads[:D].astype(F32),
        vec[6],
        sum_heads[D : 2 * D].astype(F32),
        sum_heads[2 * D :].astype(F32),
        vec[7],
        sum_out.astype(F32),
        vec[0],
        vec[1],
        vec[2],
        sum_up.astype(F32),
        small[8 * width :],
        sum_down.astype(F32),
        vec[3],
        vec[4],
        vec[5],
    )


def solution(mesh):
    in_specs = (
        P("mp", "dp"),
        P("dp"),
        P(None, "mp"),
        P("mp"),
        P(None, "mp"),
        P(None, "mp"),
        P("mp"),
        P("mp", None),
        P("mp"),
        P("mp"),
        P("mp"),
        P(None, "mp"),
        P("mp"),
        P("mp", None),
        P("mp"),
        P("mp"),
        P("mp"),
        P("mp", "dp"),
    )
    out_specs = (
        P("mp", "dp"),
        P("mp", "dp"),
        P(None, "mp"),
        P("mp"),
        P(None, "mp"),
        P(None, "mp"),
        P("mp"),
        P("mp", None),
        P("mp"),
        P("mp"),
        P("mp"),
        P(None, "mp"),
        P("mp"),
        P("mp", None),
        P("mp"),
        P("mp"),
        P("mp"),
    )
    return jax.shard_map(body, mesh=mesh, in_specs=in_specs, out_specs=out_specs, check_vma=False)
```

```python
import math

import jax
import jax.numpy as jnp
from jax import lax
from jax.experimental import pallas as pl
from jax.experimental.pallas import tpu as pltpu
from jax.sharding import PartitionSpec as P

D = 1024
HEADS = 16
HEAD = 64
SEQ_LEN = 2048

EPS = 1e-05
BIG = 1e30
Q_BLOCK = 512
K_CHUNK = 512
K_CHUNK_BACK = 256
VMEM_LIMIT = 56 * 1024 * 1024

F32 = jnp.float32
BF16 = jnp.bfloat16


def lead_dot(left, right):
    return lax.dot_general(left, right, (((0,), (0,)), ((), ())), preferred_element_type=F32)


def tail_dot(left, right):
    return lax.dot_general(left, right, (((1,), (1,)), ((), ())), preferred_element_type=F32)


def dot(left, right):
    return jnp.dot(left, right, preferred_element_type=F32)


def swap(piece, axis, mask):
    count = lax.axis_size(axis)
    return lax.ppermute(piece, axis, [(i, i ^ mask) for i in range(count)])


def bits_of(axis):
    count, found, bit = lax.axis_size(axis), [], 1
    while bit < count:
        found.append(bit)
        bit *= 2
    return found


def gather_slots(slots, axis, bits=None):
    slots = dict(slots)
    for bit in reversed(bits or bits_of(axis)):
        for slot in sorted(slots):
            slots[slot | bit] = swap(slots[slot], axis, bit)
    return slots


def slot_order(count):
    kept = [0]
    bit = count // 2
    while bit:
        kept = [slot for slot in kept] + [slot | bit for slot in kept]
        bit //= 2
    return kept


def scatter_stack(stack, axis, wire=BF16, late=None):
    for bit in bits_of(axis):
        half = stack.shape[0] // 2
        sent = stack[half:].astype(wire)
        if late is not None and bit > 1:
            sent = sent + late
        moved = swap(sent, axis, bit)
        stack = stack[:half].astype(F32) + moved.astype(F32)
    return stack


def gather_apply(own_piece, axis, apply):
    bits = bits_of(axis)
    half = own_piece.shape[1] // 2
    slots = {0: own_piece}
    for bit in reversed(bits[1:]):
        for slot in sorted(slots):
            slots[slot | bit] = swap(slots[slot], axis, bit)
    far = [slot for slot in sorted(slots) if slot]
    beside = swap(own_piece, axis, 1)
    term = apply(0, own_piece)
    term_beside = apply(2 * half, beside)
    got_beside = swap(term_beside, axis, 1)
    after, at, sums = term_beside[0, 0] * 0, 4 * half, []
    for slot in far:
        slots[slot | 1] = swap(slots[slot] + after, axis, 1)
    names = [slot for slot in sorted(slots) if slot > 1]
    done = None
    for i in range(2):
        columns = slice(i * half, (i + 1) * half)
        last = apply(at, jnp.concatenate([slots[slot][:, columns] for slot in names], axis=1))
        at += half * len(names)
        terms = {slot: last[:, k * half : (k + 1) * half] for k, slot in enumerate(names)}
        for slot in far:
            sent = terms.pop(slot | 1)
            if done is not None:
                sent = sent + done
            terms[slot] = terms[slot].astype(F32) + swap(sent, axis, 1).astype(F32)
        terms[0] = term[:, columns].astype(F32) + got_beside[:, columns].astype(F32)
        for bit in bits[1:]:
            for slot in sorted(terms, reverse=True):
                if slot & bit:
                    got = swap(terms.pop(slot).astype(BF16), axis, bit)
                    done = got[0, 0] * 0
                    terms[slot ^ bit] = terms[slot ^ bit] + got.astype(F32)
        sums.append(terms[0])
    return jnp.concatenate(sums, axis=1)


def place(slots, own, dim):
    count, width = len(slots), slots[0].shape[dim]
    shape = list(slots[0].shape)
    shape[dim] = width * count
    whole = jnp.zeros(shape, slots[0].dtype)
    for slot in sorted(slots):
        whole = lax.dynamic_update_slice_in_dim(whole, slots[slot], (own ^ slot) * width, dim)
    return whole


def cut(whole, own, slot, count, dim):
    width = whole.shape[dim] // count
    return lax.dynamic_slice_in_dim(whole, (own ^ slot) * width, width, dim)


def exchange(whole, own, axis, dim):
    count = lax.axis_size(axis)
    return {
        slot: swap(cut(whole, own, slot, count, dim), axis, slot)
        if slot
        else cut(whole, own, 0, count, dim)
        for slot in range(count)
    }


def sum_weights(piece, axis):
    index = lax.axis_index(axis)
    bits = bits_of(axis)
    groups = []
    for group in (bits[: len(bits) // 2], bits[len(bits) // 2 :]):
        masks = [0]
        for bit in group:
            masks = masks + [mask | bit for mask in masks]
        groups.append((masks, (index // (group or [1])[0]) % len(masks)))
    rows = piece.shape[0] * 2 // 3
    pieces = [piece[:rows], piece[rows:]]
    for phase in range(2):
        fresh = []
        for part in range(2):
            masks, spot = groups[phase ^ part]
            count = len(masks)
            total = cut(pieces[part], spot, 0, count, 0).astype(F32)
            for r in range(1, count):
                total = total + swap(cut(pieces[part], spot, r, count, 0), axis, masks[r]).astype(F32)
            fresh.append(total)
        zero = [(total[0, 0] * 0).astype(piece.dtype) for total in fresh]
        if phase == 0:
            begun = zero[0] + zero[1]
        pieces = [fresh[part].astype(piece.dtype) + zero[1 - part] for part in range(2)]
    for phase in (1, 0):
        fresh = []
        for part in range(2):
            masks, spot = groups[phase ^ part]
            fresh.append(
                place({r: swap(pieces[part], axis, mask) if mask else pieces[part] for r, mask in enumerate(masks)}, spot, 0)
            )
        if phase:
            zero = [whole[0, 0] * 0 for whole in fresh]
            pieces = [fresh[part] + zero[1 - part] for part in range(2)]
        else:
            pieces = fresh
    return pieces, begun


def seg_codes(segment_ids):
    digits = jnp.arange(16, dtype=jnp.int32)[:, None]
    low = (segment_ids[None, :] & 15) == digits
    high = ((segment_ids[None, :] >> 4) & 15) == digits
    same = jnp.concatenate([low, high], axis=0)
    keys = same.astype(BF16)
    queries = jnp.where(same, 0.0, -BIG).astype(BF16)
    return keys, queries


def key_ranges(segment_ids, seq_count, chunk):
    rows = segment_ids.reshape(seq_count, 1, SEQ_LEN)
    blocks = segment_ids.reshape(seq_count, SEQ_LEN // Q_BLOCK, Q_BLOCK)
    first = jnp.sum((rows < blocks[:, :, :1]).astype(jnp.int32), axis=-1)
    last = jnp.sum((rows <= blocks[:, :, -1:]).astype(jnp.int32), axis=-1)
    return (first // chunk).reshape(-1), ((last + chunk - 1) // chunk).reshape(-1)


def three_parts(row):
    lines = lax.broadcasted_iota(jnp.int32, (16, row.shape[1]), 0)
    first = row.astype(BF16).astype(F32)
    second = (row - first).astype(BF16).astype(F32)
    third = row - first - second
    spread = jnp.where(
        lines == 0, first, jnp.where(lines == 1, second, jnp.where(lines == 2, third, 0.0))
    )
    return spread.astype(BF16)


def attend_kernel(heads, from_ref, to_ref, q_ref, k_ref, v_ref, qc_ref, kc_ref, o_ref, lse_ref, kt, va, top, acc):
    seq, block = pl.program_id(0), pl.program_id(1)
    spot = seq * pl.num_programs(1) + block

    @pl.when(block == 0)
    def _():
        codes = kc_ref[...].astype(F32)
        for h in range(heads):
            rows = slice(h * HEAD, (h + 1) * HEAD)
            lines = lax.broadcasted_iota(jnp.int32, (16, SEQ_LEN), 0)
            ones = jnp.where(lines < 3, 1.0, 0.0).astype(F32)
            whole = jnp.concatenate([k_ref[rows, :].astype(F32), codes, ones, jnp.zeros_like(ones)], axis=0)
            kt[h] = whole.T.astype(BF16)
            va[h] = jnp.concatenate(
                [v_ref[rows, :], jnp.where(lines == 0, 1.0, 0.0).astype(BF16)], axis=0
            )

    top[...] = jnp.full_like(top, -BIG)
    acc[...] = jnp.zeros_like(acc)
    queries = []
    for h in range(heads):
        scaled = (q_ref[h * HEAD : (h + 1) * HEAD, :].astype(F32) * (1.0 / math.sqrt(HEAD))).astype(BF16)
        queries.append(
            jnp.concatenate([scaled, qc_ref[...], jnp.zeros((32, Q_BLOCK), BF16)], axis=0)
        )

    def highest(chunk, carry):
        at = pl.multiple_of(chunk * K_CHUNK, K_CHUNK)
        for h in range(heads):
            scores = dot(kt[h, pl.ds(at, K_CHUNK), :], queries[h])
            top[h] = jnp.maximum(top[h], jnp.max(scores.reshape(K_CHUNK // 8, 8, Q_BLOCK), axis=0))
        return carry

    lax.fori_loop(from_ref[spot], to_ref[spot], highest, 0)
    peaks, shifted = [], []
    blank = jnp.zeros((16, Q_BLOCK), BF16)
    for h in range(heads):
        peaks.append(jnp.max(top[h], axis=0, keepdims=True))
        shifted.append(
            jnp.concatenate([queries[h][:96], three_parts(-peaks[h]), blank], axis=0)
        )

    def step(chunk, carry):
        at = pl.multiple_of(chunk * K_CHUNK, K_CHUNK)
        moved = [dot(kt[h, pl.ds(at, K_CHUNK), :], shifted[h]) for h in range(heads)]
        raised = [jnp.exp(scores).astype(BF16) for scores in moved]
        for h in range(heads):
            acc[h] += dot(va[h, :, pl.ds(at, K_CHUNK)], raised[h])
        return carry

    lax.fori_loop(from_ref[spot], to_ref[spot], step, 0)
    for h in range(heads):
        total = acc[h, HEAD : HEAD + 1, :]
        o_ref[h * HEAD : (h + 1) * HEAD, :] = (acc[h, :HEAD, :] / total).astype(BF16)
        lse_ref[0, h : h + 1, :] = peaks[h] + jnp.log(total)


def attend(queries, keys, values, codes_q, codes_k, ranges, seq_count):
    width, length = queries.shape
    heads = width // HEAD
    blocks = SEQ_LEN // Q_BLOCK
    by_block = lambda s, b, *_: (0, s * blocks + b)
    by_seq = lambda s, b, *_: (0, s)
    spec = pltpu.PrefetchScalarGridSpec(
        num_scalar_prefetch=2,
        grid=(seq_count, blocks),
        in_specs=[
            pl.BlockSpec((width, Q_BLOCK), by_block),
            pl.BlockSpec((width, SEQ_LEN), by_seq),
            pl.BlockSpec((width, SEQ_LEN), by_seq),
            pl.BlockSpec((32, Q_BLOCK), by_block),
            pl.BlockSpec((32, SEQ_LEN), by_seq),
        ],
        out_specs=[
            pl.BlockSpec((width, Q_BLOCK), by_block),
            pl.BlockSpec((1, heads, Q_BLOCK), lambda s, b, *_: (0, 0, s * blocks + b)),
        ],
        scratch_shapes=[
            pltpu.VMEM((heads, SEQ_LEN, 128), BF16),
            pltpu.VMEM((heads, HEAD + 16, SEQ_LEN), BF16),
            pltpu.VMEM((heads, 8, Q_BLOCK), F32),
            pltpu.VMEM((heads, HEAD + 16, Q_BLOCK), F32),
        ],
    )
    area = length * SEQ_LEN * heads
    return pl.pallas_call(
        lambda *refs: attend_kernel(heads, *refs),
        grid_spec=spec,
        out_shape=[
            jax.ShapeDtypeStruct((width, length), BF16),
            jax.ShapeDtypeStruct((1, heads, length), F32),
        ],
        compiler_params=pltpu.CompilerParams(
            dimension_semantics=("arbitrary", "arbitrary"), vmem_limit_bytes=VMEM_LIMIT
        ),
        cost_estimate=pl.CostEstimate(flops=12 * HEAD * area, bytes_accessed=8 * width * length, transcendentals=area),
        name="attend",
    )(*ranges, queries, keys, values, codes_q, codes_k)


def attend_back_kernel(
    heads, from_ref, to_ref, q_ref, o_ref, do_ref, lse_ref, k_ref, v_ref, qc_ref, kc_ref, out_ref, kt, vt, acc, dq_acc
):
    seq, block = pl.program_id(0), pl.program_id(1)
    spot = seq * pl.num_programs(1) + block

    @pl.when(block == 0)
    def _():
        codes = kc_ref[...].astype(F32)
        lines = lax.broadcasted_iota(jnp.int32, (16, SEQ_LEN), 0)
        ones = jnp.where(lines < 3, 1.0, 0.0).astype(F32)
        blank = jnp.zeros((16, SEQ_LEN), F32)
        for h in range(heads):
            rows = slice(h * HEAD, (h + 1) * HEAD)
            kt[h] = jnp.concatenate([k_ref[rows, :].astype(F32), codes, ones, blank], axis=0).T.astype(BF16)
            vt[h] = jnp.concatenate([v_ref[rows, :].astype(F32), ones, blank, blank, blank], axis=0).T.astype(BF16)
        acc[...] = jnp.zeros_like(acc)

    dq_acc[...] = jnp.zeros_like(dq_acc)
    lanes = lax.broadcasted_iota(jnp.int32, (Q_BLOCK, 128), 1)
    blank = jnp.zeros((16, Q_BLOCK), BF16)

    queries, grads, both = [], [], []
    for h in range(heads):
        rows = slice(h * HEAD, (h + 1) * HEAD)
        scaled = q_ref[rows, :].astype(F32) * (1.0 / math.sqrt(HEAD))
        grad = do_ref[rows, :].astype(F32)
        centre = jnp.sum(grad * o_ref[rows, :].astype(F32), axis=0, keepdims=True)
        queries.append(
            jnp.concatenate([scaled.astype(BF16), qc_ref[...], three_parts(-lse_ref[0, h : h + 1, :]), blank], axis=0)
        )
        grads.append(jnp.concatenate([do_ref[rows, :], three_parts(-centre), blank, blank, blank], axis=0))
        turned = jnp.concatenate([grad, scaled], axis=0).T
        both.append(
            jnp.concatenate(
                [jnp.where(lanes < HEAD, turned, 0.0), jnp.where(lanes < HEAD, 0.0, turned)], axis=0
            ).astype(BF16)
        )

    def step(chunk, carry):
        span = pl.ds(pl.multiple_of(chunk * K_CHUNK_BACK, K_CHUNK_BACK), K_CHUNK_BACK)
        for h in range(heads):
            softened = jnp.exp(dot(kt[h, span, :], queries[h]))
            shifted = dot(vt[h, span, :], grads[h])
            score_grad = (softened * shifted).astype(BF16)
            pair = jnp.concatenate([softened.astype(BF16), score_grad], axis=1)
            acc[h, span, :] += dot(pair, both[h])
            dq_acc[h] += dot(k_ref[h * HEAD : (h + 1) * HEAD, span], score_grad)
        return carry

    lax.fori_loop(from_ref[spot], to_ref[spot], step, 0)
    query_rows = [None] * heads
    for h in range(heads):
        query_rows[h] = dq_acc[h] * (1.0 / math.sqrt(HEAD))
    own_rows = pl.ds(pl.multiple_of(block * Q_BLOCK, Q_BLOCK), Q_BLOCK)
    out_ref[own_rows, 2 * heads * HEAD :] = jnp.concatenate(query_rows, axis=0).T.astype(BF16)

    @pl.when(block == pl.num_programs(1) - 1)
    def _():
        out_ref[:, : heads * HEAD] = jnp.concatenate(
            [acc[h, :, :HEAD] for h in range(heads)], axis=1
        ).astype(BF16)
        out_ref[:, heads * HEAD : 2 * heads * HEAD] = jnp.concatenate(
            [acc[h, :, HEAD:] for h in range(heads)], axis=1
        ).astype(BF16)


def attend_back(queries, context, grads, log_totals, keys, values, codes_q, codes_k, ranges, seq_count):
    width, length = queries.shape
    heads = width // HEAD
    blocks = SEQ_LEN // Q_BLOCK
    by_block = lambda s, b, *_: (0, s * blocks + b)
    by_seq = lambda s, b, *_: (0, s)
    spec = pltpu.PrefetchScalarGridSpec(
        num_scalar_prefetch=2,
        grid=(seq_count, blocks),
        in_specs=[
            pl.BlockSpec((width, Q_BLOCK), by_block),
            pl.BlockSpec((width, Q_BLOCK), by_block),
            pl.BlockSpec((width, Q_BLOCK), by_block),
            pl.BlockSpec((1, heads, Q_BLOCK), lambda s, b, *_: (0, 0, s * blocks + b)),
            pl.BlockSpec((width, SEQ_LEN), by_seq),
            pl.BlockSpec((width, SEQ_LEN), by_seq),
            pl.BlockSpec((32, Q_BLOCK), by_block),
            pl.BlockSpec((32, SEQ_LEN), by_seq),
        ],
        out_specs=pl.BlockSpec((SEQ_LEN, 3 * width), lambda s, b, *_: (s, 0)),
        scratch_shapes=[
            pltpu.VMEM((heads, SEQ_LEN, 128), BF16),
            pltpu.VMEM((heads, SEQ_LEN, 128), BF16),
            pltpu.VMEM((heads, SEQ_LEN, 128), F32),
            pltpu.VMEM((heads, HEAD, Q_BLOCK), F32),
        ],
    )
    area = length * SEQ_LEN * heads
    return pl.pallas_call(
        lambda *refs: attend_back_kernel(heads, *refs),
        grid_spec=spec,
        out_shape=jax.ShapeDtypeStruct((length, 3 * width), BF16),
        compiler_params=pltpu.CompilerParams(
            dimension_semantics=("arbitrary", "arbitrary"), vmem_limit_bytes=VMEM_LIMIT
        ),
        cost_estimate=pl.CostEstimate(flops=30 * HEAD * area, bytes_accessed=14 * width * length, transcendentals=area),
        name="attend_back",
    )(*ranges, queries, context, grads, log_totals, keys, values, codes_q, codes_k)


TOKEN_BLOCK = 256


def feed_kernel(y_ref, up_ref, bias_ref, down_ref, *refs):
    y_out, g_ref, slope_ref, part_ref = refs[-4:]
    hidden = up_ref.shape[0]
    piece = min(256, hidden)
    total = None
    y_out[...] = y_ref[...]
    for at in range(0, hidden, piece):
        rows = slice(at, at + piece)
        upward = dot(up_ref[rows, :], y_ref[...]) + bias_ref[rows, :]
        flat = (1.0 + lax.erf(upward * (1.0 / math.sqrt(2.0)))) * 0.5
        slope = flat + upward * jnp.exp(upward * upward * -0.5) * (1.0 / math.sqrt(2.0 * math.pi))
        active = (upward * flat).astype(BF16)
        g_ref[rows, :] = active
        slope_ref[rows, :] = slope.astype(BF16)
        term = dot(down_ref[:, rows], active)
        total = term if total is None else total + term
    part_ref[...] = total.astype(part_ref.dtype)


def feed(at, total, kept, first_low, up_turned, bias_up, down_turned):
    tokens = first_low.shape[1]
    hidden = up_turned.shape[0]
    blocks = tokens // TOKEN_BLOCK
    by_token = lambda t: (0, t)
    in_whole = lambda t: (0, at // TOKEN_BLOCK + t)
    whole = lambda t: (0, 0)
    *kept, part = pl.pallas_call(
        feed_kernel,
        grid=(blocks,),
        in_specs=[
            pl.BlockSpec((D, TOKEN_BLOCK), by_token),
            pl.BlockSpec((hidden, D), whole),
            pl.BlockSpec((hidden, 1), whole),
            pl.BlockSpec((D, hidden), whole),
        ]
        + [pl.BlockSpec(memory_space=pl.ANY)] * len(kept),
        out_specs=[
            pl.BlockSpec((D, TOKEN_BLOCK), in_whole),
            pl.BlockSpec((hidden, TOKEN_BLOCK), in_whole),
            pl.BlockSpec((hidden, TOKEN_BLOCK), in_whole),
            pl.BlockSpec((D, TOKEN_BLOCK), by_token),
        ],
        out_shape=[
            jax.ShapeDtypeStruct((D, total), BF16),
            jax.ShapeDtypeStruct((hidden, total), BF16),
            jax.ShapeDtypeStruct((hidden, total), BF16),
            jax.ShapeDtypeStruct((D, tokens), BF16),
        ],
        input_output_aliases={4 + i: i for i in range(len(kept))},
        compiler_params=pltpu.CompilerParams(
            dimension_semantics=("arbitrary",), vmem_limit_bytes=VMEM_LIMIT
        ),
        cost_estimate=pl.CostEstimate(
            flops=4 * D * hidden * tokens, bytes_accessed=4 * D * hidden + 8 * D * tokens, transcendentals=2 * hidden * tokens
        ),
        name="feed",
    )(first_low, up_turned, bias_up, down_turned, *kept)
    return kept, part


def feed_back_kernel(m_ref, slope_ref, down_ref, up_ref, *refs):
    m_out, du_ref, part_ref = refs[-3:]
    hidden = down_ref.shape[0]
    piece = min(256, hidden)
    total = None
    m_out[...] = m_ref[...]
    for at in range(0, hidden, piece):
        rows = slice(at, at + piece)
        grad = (dot(down_ref[rows, :], m_ref[...]) * slope_ref[rows, :].astype(F32)).astype(BF16)
        du_ref[rows, :] = grad
        term = dot(up_ref[:, rows], grad)
        total = term if total is None else total + term
    part_ref[...] = total.astype(part_ref.dtype)


def feed_back(at, total, kept, down_low, slope, w_down, w_up):
    tokens = down_low.shape[1]
    hidden = w_down.shape[0]
    blocks = tokens // TOKEN_BLOCK
    by_token = lambda t: (0, t)
    in_whole = lambda t: (0, at // TOKEN_BLOCK + t)
    whole = lambda t: (0, 0)
    *kept, part = pl.pallas_call(
        feed_back_kernel,
        grid=(blocks,),
        in_specs=[
            pl.BlockSpec((D, TOKEN_BLOCK), by_token),
            pl.BlockSpec((hidden, TOKEN_BLOCK), in_whole),
            pl.BlockSpec((hidden, D), whole),
            pl.BlockSpec((D, hidden), whole),
        ]
        + [pl.BlockSpec(memory_space=pl.ANY)] * len(kept),
        out_specs=[
            pl.BlockSpec((D, TOKEN_BLOCK), in_whole),
            pl.BlockSpec((hidden, TOKEN_BLOCK), in_whole),
            pl.BlockSpec((D, TOKEN_BLOCK), by_token),
        ],
        out_shape=[
            jax.ShapeDtypeStruct((D, total), BF16),
            jax.ShapeDtypeStruct((hidden, total), BF16),
            jax.ShapeDtypeStruct((D, tokens), BF16),
        ],
        input_output_aliases={4 + i: i for i in range(len(kept))},
        compiler_params=pltpu.CompilerParams(
            dimension_semantics=("arbitrary",), vmem_limit_bytes=VMEM_LIMIT
        ),
        cost_estimate=pl.CostEstimate(
            flops=4 * D * hidden * tokens, bytes_accessed=4 * D * hidden + 8 * D * tokens, transcendentals=0
        ),
        name="feed_back",
    )(down_low, slope, w_down, w_up, *kept)
    return kept, part


def norm_rows(values, norm_gain, norm_shift):
    centre = values - jnp.mean(values, axis=0, keepdims=True)
    inverse = lax.rsqrt(jnp.mean(centre * centre, axis=0, keepdims=True) + EPS)
    normed = centre * inverse
    return (normed * norm_gain[:, None] + norm_shift[:, None], normed, inverse)


def norm_back(grad_rows, normed, inverse, norm_gain):
    scaled = grad_rows * norm_gain[:, None]
    return inverse * (
        scaled
        - jnp.mean(scaled, axis=0, keepdims=True)
        - normed * jnp.mean(scaled * normed, axis=0, keepdims=True)
    )


def body(
    hidden_in,
    segment_ids,
    w_query,
    b_query,
    w_key,
    w_value,
    b_value,
    w_out,
    b_out,
    gain_one,
    shift_one,
    w_up,
    b_up,
    w_down,
    b_down,
    gain_two,
    shift_two,
    cotangent,
):
    parts = lax.axis_size("mp")
    own = lax.axis_index("mp")
    width, length = hidden_in.shape
    seq_count = length // SEQ_LEN
    own_len = length // parts
    own_heads = width // HEAD

    input_slots = gather_slots({0: hidden_in}, "mp")
    inputs = place(input_slots, own, 0)
    after = input_slots[parts // 2][0, 0] * 0
    vectors = jnp.stack([b_out, gain_one, shift_one, b_down, gain_two, shift_two])
    vectors = place(gather_slots({0: vectors}, "mp"), own, 1).astype(F32)
    bias_out, gain_first, shift_first, bias_down, gain_second, shift_second = [vectors[i] for i in range(6)]
    out_slots = gather_slots({0: w_out + after}, "mp", bits_of("mp")[1:])
    cot_own = place(exchange(cotangent, own + after.astype(jnp.int32), "mp", 1), own, 0)
    up_turned, down_turned = w_up.T, w_down.T
    order = slot_order(parts)

    w_three = jnp.concatenate([w_value, w_key, w_query], axis=1)
    biases = jnp.concatenate([b_value, jnp.zeros_like(b_query), b_query]).astype(F32)[:, None]
    projected = (dot(w_three.T, inputs) + biases).astype(BF16)
    values, keys, queries = projected[:width], projected[width : 2 * width], projected[2 * width :]
    w_slots = jnp.concatenate([cut(w_three, own, r, parts, 0) for r in order], axis=0)
    codes_k, codes_q = seg_codes(segment_ids)
    ranges = key_ranges(segment_ids, seq_count, K_CHUNK)
    ranges_back = key_ranges(segment_ids, seq_count, K_CHUNK_BACK)
    context, log_totals = attend(queries, keys, values, codes_q, codes_k, ranges, seq_count)

    out_slots = {slot: piece + context[0, 0] * 0 if slot else piece for slot, piece in out_slots.items()}
    out_slots = gather_slots(out_slots, "mp", [1])
    full_out = jnp.concatenate([out_slots[r] for r in range(parts)], axis=0)

    context_slots = exchange(context, own, "mp", 1)
    context_own = jnp.concatenate([context_slots[r] for r in range(parts)], axis=0)
    inputs_own = lax.dynamic_slice_in_dim(inputs, own * own_len, own_len, 1)
    first_sum = inputs_own.astype(F32) + (lead_dot(full_out, context_own) + bias_out[:, None])
    first_out, normed_first, inverse_one = norm_rows(first_sum, gain_first, shift_first)

    bias_up = b_up.astype(F32)[:, None]
    kept = []

    def forth(at, piece):
        kept[:], part = feed(at, length, list(kept), piece, up_turned, bias_up, down_turned)
        return part

    fed = gather_apply(first_out.astype(BF16), "mp", forth)
    all_first, all_active, all_slope = kept
    second_sum = first_out + (fed + bias_down[:, None])
    final_rows, normed_second, inverse_two = norm_rows(second_sum, gain_second, shift_second)

    grad_rows = cot_own.astype(F32)
    grad_shift_two = jnp.sum(grad_rows, axis=1)
    grad_gain_two = jnp.sum(grad_rows * normed_second, axis=1)
    second_grad = norm_back(grad_rows, normed_second, inverse_two, gain_second)
    grad_b_down = jnp.sum(second_grad, axis=1)

    kept_back = []

    def back(at, piece):
        kept_back[:], part = feed_back(at, length, list(kept_back), piece, all_slope, w_down, w_up)
        return part

    fed_back = gather_apply(second_grad.astype(BF16), "mp", back)
    all_down, all_up = kept_back
    grad_w_down = tail_dot(all_active, all_down).astype(BF16)
    grad_w_up = tail_dot(all_first, all_up).astype(BF16)
    grad_b_up = jnp.sum(all_up.astype(F32), axis=1)
    sum_down, sum_up = lax.psum((grad_w_down, grad_w_up), "dp")

    first_grad = second_grad + fed_back
    grad_shift_one = jnp.sum(first_grad, axis=1)
    grad_gain_one = jnp.sum(first_grad * normed_first, axis=1)
    attn_grad = norm_back(first_grad, normed_first, inverse_one, gain_first)
    grad_b_out = jnp.sum(attn_grad, axis=1)
    out_low = attn_grad.astype(BF16)
    context_grad = dot(full_out, out_low).astype(BF16)
    grad_heads = place(
        {r: swap(context_grad[r * width : (r + 1) * width], "mp", r) if r else context_grad[:width] for r in range(parts)},
        own,
        1,
    )
    late = grad_heads[0, 0] * 0
    final_low = final_rows.astype(BF16) + late
    twice = jnp.concatenate([final_low.reshape(parts, width, own_len), out_low.reshape(parts, width, own_len)], axis=1)
    back_here = place(exchange(twice.reshape(2 * D, own_len), own, "mp", 0), own, 1)
    layer_out, attn_here = back_here[:width], back_here[width:]
    stack_of = lambda slots: jnp.concatenate([slots[r] for r in order], axis=0)
    out_part = tail_dot(stack_of(context_slots), out_low).astype(BF16)
    grad_w_out = scatter_stack(out_part, "mp").astype(BF16)
    mixed = jnp.stack([grad_b_out, grad_gain_one, grad_shift_one, grad_b_down, grad_gain_two, grad_shift_two])
    mixed = scatter_stack(stack_of({r: cut(mixed, own, r, parts, 1) for r in range(parts)}), "mp", wire=F32)

    ready = (grad_w_down[0, 0] + grad_w_up[0, 0]) * 0
    all_grad = attend_back(
        queries, context, grad_heads + ready, log_totals, keys, values, codes_q, codes_k, ranges_back, seq_count
    )
    grad_biases = jnp.sum(all_grad.astype(F32), axis=0)
    grad_three = dot(inputs, all_grad)
    mixed = mixed + (back_here[0, 0] * 0).astype(F32)
    small = jnp.concatenate([mixed.reshape(-1), grad_biases[2 * width :], grad_biases[:width], grad_b_up])
    columns = 4 * width
    rows_small = 128
    small = jnp.concatenate([small, jnp.zeros((rows_small * columns - small.shape[0],), F32)]).reshape(rows_small, columns)
    packed = jnp.concatenate(
        [
            jnp.concatenate([grad_three.astype(BF16), grad_w_out.reshape(D, width)], axis=1),
            small.astype(BF16),
        ],
        axis=0,
    )
    input_part = tail_dot(w_slots + packed[0, 0] * 0, all_grad).astype(BF16)
    pieces, begun = sum_weights(packed, "dp")
    input_grad = (scatter_stack(input_part, "mp", late=begun) + attn_here.astype(F32)).astype(BF16)
    packed = jnp.concatenate(pieces, axis=0).astype(F32)
    small = packed[D:].reshape(-1)
    vec = [small[i * width : (i + 1) * width] for i in range(8)]
    sum_value, sum_key, sum_query = [packed[:D, i * width : (i + 1) * width] for i in range(3)]
    sum_out = packed[:D, 3 * width :].reshape(width, D)
    return (
        layer_out,
        input_grad,
        sum_query,
        vec[6],
        sum_key,
        sum_value,
        vec[7],
        sum_out,
        vec[0],
        vec[1],
        vec[2],
        sum_up.astype(F32),
        small[8 * width : 12 * width],
        sum_down.astype(F32),
        vec[3],
        vec[4],
        vec[5],
    )


def solution(mesh):
    in_specs = (
        P("mp", "dp"),
        P("dp"),
        P(None, "mp"),
        P("mp"),
        P(None, "mp"),
        P(None, "mp"),
        P("mp"),
        P("mp", None),
        P("mp"),
        P("mp"),
        P("mp"),
        P(None, "mp"),
        P("mp"),
        P("mp", None),
        P("mp"),
        P("mp"),
        P("mp"),
        P("mp", "dp"),
    )
    out_specs = (
        P("mp", "dp"),
        P("mp", "dp"),
        P(None, "mp"),
        P("mp"),
        P(None, "mp"),
        P(None, "mp"),
        P("mp"),
        P("mp", None),
        P("mp"),
        P("mp"),
        P("mp"),
        P(None, "mp"),
        P("mp"),
        P("mp", None),
        P("mp"),
        P("mp"),
        P("mp"),
    )
    return jax.shard_map(body, mesh=mesh, in_specs=in_specs, out_specs=out_specs, check_vma=False)
```
